256 devices in a mesh: gx: 16 (over z, y_lo), gy: 16 (over y_hi, x, core).
Axes of the slice: x: 4, y: 4 (y_hi: 2, y_lo: 2; y = y_hi * 2 + y_lo), z: 8, core: 2. Of those that a mesh axis runs over, the one named last changes fastest.
Arguments:
- snapshot_panel: float32 [64, 524288], P(None, ('gx', 'gy')), may hold values from -2500 to 2500, as said below
- following: float32 [960, 524288], P(None, ('gx', 'gy')), may hold values from -2500 to 2500, as said below
Outputs:
- basis_rows: float32 [64, 524288], P(None, ('gx', 'gy'))
- upper_factor: float32 [64, 64], replicated
- projection: float32 [64, 960], replicated
The draws below stay inside these ranges and needn't reach their ends.
Inputs may be any that keep to these rules, and one draw needn't show every extreme that they name: `snapshot_panel`: real-valued snapshots of full rank. `following`: real-valued snapshots.
All inputs are finite; a program needn't handle non-finite values.
Results may differ from the reference program's by a relative error of at most 0.000077.
Values sent between devices are 32-bit elements; how exact they have to be, the bound alone decides.
No kernel may reach another device: no remote copies, remote signals or barrier semaphores. Data moves between devices by JAX's collectives and lax.ppermute only.
A program may use at most 64 MiB of HBM per device.

```python
import math
import jax
import jax.numpy as jnp
from jax import lax

P_SIZE = 64
NEXT = 960
ROWS = 524288


def common_parts(key, spread_log):
    keys = jax.random.split(key, 4)
    normal_part = jax.random.truncated_normal(keys[0], -4.0, 4.0, (P_SIZE, ROWS), jnp.float32)
    position = jnp.arange(ROWS, dtype=jnp.float32) / ROWS
    row_scale = (1.0 + 2.0 * position) * jnp.exp(jax.random.uniform(keys[2], (ROWS,), jnp.float32) * spread_log)
    col_scale = jnp.exp(jax.random.uniform(keys[3], (P_SIZE, 1), jnp.float32) * math.log(10.0))
    return (normal_part * col_scale, row_scale[None, :])


def draw_snapshot_panel(key, part):
    columns, row_scale = common_parts(key, math.log(3.0))
    return (columns * row_scale).astype(jnp.float32)


def draw_following(key, part):
    columns, row_scale = common_parts(key, math.log(3.0))
    own_key = jax.random.fold_in(key, 7)
    noise_key, scale_key = jax.random.split(own_key, 2)
    noise = jax.random.truncated_normal(noise_key, -4.0, 4.0, (NEXT, ROWS), jnp.float32)
    noise_scale = jnp.exp(jax.random.uniform(scale_key, (NEXT, 1), jnp.float32) * math.log(10.0))
    repeated = jnp.tile(columns, (NEXT // P_SIZE, 1))
    return (row_scale * (0.6 * repeated + noise * noise_scale)).astype(jnp.float32)


def setup_inputs(seed: int = 0) -> dict:
    arg_keys = jax.random.split(jax.random.key(seed), 3)
    snapshot_panel = draw_snapshot_panel(jax.random.fold_in(arg_keys[2], 71), 0)
    following = draw_following(jax.random.fold_in(arg_keys[2], 71), 0)
    return dict(snapshot_panel=snapshot_panel, following=following)


def inner_product(left, right):
    return lax.dot_general(left.astype(jnp.float32), right.astype(jnp.float32), (((1,), (1,)), ((), ())), precision=lax.Precision.HIGHEST, preferred_element_type=jnp.float32)

def reference(snapshot_panel, following):
    gram_matrix = inner_product(snapshot_panel, snapshot_panel)
    lower_factor = jnp.linalg.cholesky(gram_matrix)
    cross_terms = inner_product(snapshot_panel, following)
    root_rows = math.sqrt(ROWS)
    basis_rows = jax.scipy.linalg.solve_triangular(lower_factor, snapshot_panel, lower=True) * root_rows
    upper_factor = lower_factor.T / root_rows
    projection = jax.scipy.linalg.solve_triangular(lower_factor, cross_terms, lower=True) / root_rows
    return (basis_rows, upper_factor, projection)
```

```python
import math

import jax
import jax.numpy as jnp
import numpy as np
from jax import lax
from jax.experimental import pallas as pl
from jax.experimental.pallas import tpu as pltpu
from jax.sharding import PartitionSpec as P

AXES = ("gx", "gy")
SIZES = (8, 2, 2, 4, 2)
LAST = (((1,), (1,)), ((), ()))
MIB = 1 << 20


def route(place, core=None):
    pairs = []
    for index, (z, y_lo, y_hi, x, c) in enumerate(np.ndindex(*SIZES)):
        if core is None or c == core:
            tz, ty, tx, tc = place(z, 2 * y_hi + y_lo, x, c)
            pairs.append((index, int(np.ravel_multi_index((tz, ty % 2, ty // 2, tx, tc), SIZES))))
    return pairs


def x_flip(mask):
    return lambda z, y, x, c: (z, y, x ^ mask, c)


def y_flip(mask):
    return lambda z, y, x, c: (z, y ^ mask, x, c)


def z_flip(mask):
    return lambda z, y, x, c: (z ^ mask, y, x, c)


def core_flip(z, y, x, c):
    return (z, y, x, c ^ 1)


def summed(blocks, cores, flips):
    blocks = [b + lax.ppermute(b, AXES, route(core_flip, 1 - c)) for b, c in zip(blocks, cores)]
    for flip in zip(*flips):
        blocks = [b + lax.ppermute(b, AXES, route(f, c)) for b, c, f in zip(blocks, cores, flip)]
        blocks[:2] = lax.optimization_barrier(blocks[:2])
    core = lax.axis_index("gy") % 2
    return [jnp.where(core == c, b, lax.ppermute(b, AXES, route(core_flip, c))) for b, c in zip(blocks, cores)]


def parts3(values):
    high = values.astype(jnp.bfloat16)
    rest = values - high.astype(jnp.float32)
    middle = rest.astype(jnp.bfloat16)
    return high, middle, (rest - middle.astype(jnp.float32)).astype(jnp.bfloat16)


def last_product(left, right):
    return lax.dot_general(left, right, LAST, preferred_element_type=jnp.float32)


def local_products(panel, following):
    width, cells = panel.shape
    count = following.shape[0]
    half = 512
    pieces = 4
    piece = cells // pieces

    def kernel(panel_hbm, following_hbm, gram_ref, first_ref, second_ref, panel_v, following_v, stack, total, sem):
        panel_copy = pltpu.make_async_copy(panel_hbm, panel_v, sem.at[0])
        panel_copy.start()
        copies = []
        for i in range(pieces):
            columns = pl.ds(i * piece, piece)
            copies.append(
                pltpu.make_async_copy(following_hbm.at[:, columns], following_v.at[:, columns], sem.at[1 + i])
            )
            copies[-1].start()
        panel_copy.wait()
        high, middle, low = parts3(panel_v[...])
        stack[0:width] = high
        stack[width : 2 * width] = middle
        stack[2 * width :] = low
        whole = stack[...]
        sums = last_product(whole, high) + last_product(whole, middle) + last_product(whole, low)
        gram = sums[:width] + sums[width : 2 * width] + sums[2 * width :]
        gram_ref[:, :width] = gram[: width // 2]
        gram_ref[:, width:] = gram[width // 2 :]
        for i in range(pieces):
            copies[i].wait()
            columns = slice(i * piece, (i + 1) * piece)
            values = following_v[:, columns]
            high = values.astype(jnp.bfloat16)
            low = (values - high.astype(jnp.float32)).astype(jnp.bfloat16)
            part = stack[:, columns]
            sums = last_product(part, high) + last_product(part, low)
            if i:
                total[...] += sums
            else:
                total[...] = sums
        cross = total[:width] + total[width : 2 * width] + total[2 * width :]
        first_ref[...] = cross[:, :half]
        second_ref[...] = cross[:, half:]

    return pl.pallas_call(
        kernel,
        out_shape=(
            jax.ShapeDtypeStruct((width // 2, 2 * width), jnp.float32),
            jax.ShapeDtypeStruct((width, half), jnp.float32),
            jax.ShapeDtypeStruct((width, count - half), jnp.float32),
        ),
        in_specs=[pl.BlockSpec(memory_space=pl.ANY)] * 2,
        out_specs=(pl.BlockSpec(memory_space=pltpu.VMEM),) * 3,
        scratch_shapes=[
            pltpu.VMEM((width, cells), jnp.float32),
            pltpu.VMEM((count, cells), jnp.float32),
            pltpu.VMEM((3 * width, cells), jnp.bfloat16),
            pltpu.VMEM((3 * width, count), jnp.float32),
            pltpu.SemaphoreType.DMA((1 + pieces,)),
        ],
        compiler_params=pltpu.CompilerParams(vmem_limit_bytes=56 * MIB),
        name="local_products",
    )(panel, following)


def factor(gram, panel, root_rows):
    width, cells = panel.shape

    def kernel(gram_ref, panel_ref, upper_ref, inverse_ref, basis_ref):
        rows = lax.broadcasted_iota(jnp.int32, (width, 2 * width), 0)
        lanes = lax.broadcasted_iota(jnp.int32, (width, 2 * width), 1)
        whole = jnp.concatenate([gram_ref[:, :width], gram_ref[:, width:]], axis=0)
        unit = (rows[:, :width] == lanes[:, :width]).astype(jnp.float32)
        work = jnp.concatenate([whole, unit], axis=1)
        for k in range(width - 1):
            row = work[k : k + 1, :]
            column = jnp.broadcast_to(work[:, k : k + 1], (width, 2 * width))
            pivot = column[k : k + 1, :]
            work = work - jnp.where(rows > k, column, 0.0) * (row / pivot)
        pivots = jnp.sum(jnp.where(rows == lanes, work, 0.0), axis=1, keepdims=True)
        work = work / jnp.sqrt(pivots)
        upper = work[:, :width]
        inverse = work[:, width:]
        upper_ref[...] = jnp.where(rows[:, :width] <= lanes[:, :width], upper, 0.0) * (1.0 / root_rows)
        inverse_ref[...] = inverse * (1.0 / root_rows)
        lh, lm, ll = parts3(inverse * root_rows)
        ph, pm, po = parts3(panel_ref[...])
        left = jnp.concatenate([lh, lh, lh, lm, lm, ll], axis=1)
        right = jnp.concatenate([ph, pm, po, ph, pm, ph], axis=0)
        basis_ref[...] = jnp.dot(left, right, preferred_element_type=jnp.float32)

    return pl.pallas_call(
        kernel,
        out_shape=(
            jax.ShapeDtypeStruct((width, width), jnp.float32),
            jax.ShapeDtypeStruct((width, width), jnp.float32),
            jax.ShapeDtypeStruct((width, cells), jnp.float32),
        ),
        compiler_params=pltpu.CompilerParams(vmem_limit_bytes=32 * MIB),
        name="factor",
    )(gram, panel)


def body(snapshot_panel, following):
    root_rows = math.sqrt(snapshot_panel.shape[1] * lax.axis_size(AXES))
    gram, first, second = local_products(snapshot_panel, following)
    mirror = z_flip(7)
    near = [x_flip(1), x_flip(2), y_flip(1), y_flip(2), mirror, z_flip(1), z_flip(2)]
    one = [x_flip(1), x_flip(3), y_flip(1), y_flip(3), mirror, z_flip(1), z_flip(2)]
    two = [z_flip(1), z_flip(2), mirror, y_flip(1), y_flip(3), x_flip(1), x_flip(3)]
    gram, first, second = summed([gram, first, second], [0, 1, 1], [near, one, two])
    upper, inverse, basis = factor(gram, snapshot_panel, root_rows)
    cross = jnp.concatenate([first, second], axis=1)
    projection = jnp.dot(inverse, cross, precision=lax.Precision.HIGHEST, preferred_element_type=jnp.float32)
    return basis, upper, projection


def solution(mesh):
    return jax.shard_map(
        body,
        mesh=mesh,
        in_specs=(P(None, AXES), P(None, AXES)),
        out_specs=(P(None, AXES), P(), P()),
        check_vma=False,
    )
```

```python
import math

import jax
import jax.numpy as jnp
from jax import lax
from jax.experimental import pallas as pl
from jax.experimental.pallas import tpu as pltpu
from jax.sharding import Mesh
from jax.sharding import PartitionSpec as P

AXES = ("z", "y_lo", "y_hi", "x", "core")
SIZES = (8, 2, 2, 4, 2)
PLANE = AXES[1:]
LAST = (((1,), (1,)), ((), ()))
LANES = 128
MIB = 1 << 20
BLOCK = 8


def parts3(values):
    high = values.astype(jnp.bfloat16)
    rest = values - high.astype(jnp.float32)
    middle = rest.astype(jnp.bfloat16)
    return high, middle, (rest - middle.astype(jnp.float32)).astype(jnp.bfloat16)


def last_product(left, right):
    return lax.dot_general(left, right, LAST, preferred_element_type=jnp.float32)


def local_products(panel, following):
    width, cells = panel.shape
    count = following.shape[0]
    columns = count + width
    pieces = 4
    piece = cells // pieces

    def kernel(panel_hbm, following_hbm, out_ref, panel_v, following_v, stack, total, sem):
        panel_copy = pltpu.make_async_copy(panel_hbm, panel_v, sem.at[0])
        panel_copy.start()
        copies = []
        for i in range(pieces):
            cut = pl.ds(i * piece, piece)
            copies.append(pltpu.make_async_copy(following_hbm.at[:, cut], following_v.at[:, cut], sem.at[1 + i]))
            copies[-1].start()
        panel_copy.wait()
        high, middle, low = parts3(panel_v[...])
        stack[0:width] = high
        stack[width : 2 * width] = middle
        stack[2 * width :] = low
        whole = stack[...]
        sums = last_product(whole, high) + last_product(whole, middle) + last_product(whole, low)
        gram = sums[:width] + sums[width : 2 * width] + sums[2 * width :]
        for i in range(pieces):
            copies[i].wait()
            cut = slice(i * piece, (i + 1) * piece)
            values = following_v[:, cut]
            high = values.astype(jnp.bfloat16)
            low = (values - high.astype(jnp.float32)).astype(jnp.bfloat16)
            part = stack[:, cut]
            sums = last_product(part, high) + last_product(part, low)
            if i:
                total[...] += sums
            else:
                total[...] = sums
        cross = total[:width] + total[width : 2 * width] + total[2 * width :]
        both = jnp.concatenate([cross, gram], axis=1)
        for j in range(columns // LANES):
            out_ref[j * width : (j + 1) * width] = both[:, j * LANES : (j + 1) * LANES]

    return pl.pallas_call(
        kernel,
        out_shape=jax.ShapeDtypeStruct((width * columns // LANES, LANES), jnp.float32),
        in_specs=[pl.BlockSpec(memory_space=pl.ANY)] * 2,
        out_specs=pl.BlockSpec(memory_space=pltpu.VMEM),
        scratch_shapes=[
            pltpu.VMEM((width, cells), jnp.float32),
            pltpu.VMEM((count, cells), jnp.float32),
            pltpu.VMEM((3 * width, cells), jnp.bfloat16),
            pltpu.VMEM((3 * width, count), jnp.float32),
            pltpu.SemaphoreType.DMA((1 + pieces,)),
        ],
        compiler_params=pltpu.CompilerParams(vmem_limit_bytes=60 * MIB),
        name="local_products",
    )(panel, following)


def eliminated(work, width):
    done = []
    for base in range(0, width, BLOCK):
        left = width - base
        columns = [jnp.broadcast_to(work[:, base + j : base + j + 1], (left, 2 * width)) for j in range(BLOCK)]
        rows = [work[j : j + 1] for j in range(BLOCK)]
        corner = [[columns[j][i : i + 1] for j in range(BLOCK)] for i in range(BLOCK)]
        inverses = []
        for j in range(BLOCK):
            inverses.append(1.0 / corner[j][j])
            for i in range(j + 1, BLOCK):
                factor = corner[i][j] * inverses[j]
                rows[i] = rows[i] - factor * rows[j]
                for k in range(j + 1, BLOCK):
                    corner[i][k] = corner[i][k] - factor * corner[j][k]
        if left > BLOCK:
            below = [column[BLOCK:] for column in columns]
            work = work[BLOCK:]
            for j in range(BLOCK):
                work = work - below[j] * (rows[j] * inverses[j])
                for k in range(j + 1, BLOCK):
                    below[k] = below[k] - below[j] * (corner[j][k] * inverses[j])
        done += [rows[j] / jnp.sqrt(corner[j][j]) for j in range(BLOCK)]
    return jnp.concatenate(done, axis=0)


def results(summed, panel, root_rows):
    width, cells = panel.shape
    count = summed.shape[0] * LANES // width - width

    def kernel(summed_ref, panel_ref, basis_ref, upper_ref, projection_ref):
        rows = lax.broadcasted_iota(jnp.int32, (width, 2 * width), 0)
        lanes = lax.broadcasted_iota(jnp.int32, (width, 2 * width), 1)
        gram_last = summed_ref[summed_ref.shape[0] - width :]
        unit = jnp.where(lanes == rows + width, 1.0, 0.0)
        work = eliminated(jnp.where(lanes < width, pltpu.roll(gram_last, width, axis=1), unit), width)
        upper_ref[...] = jnp.where(rows <= lanes, work, 0.0)[:, :width] * (1.0 / root_rows)
        high, middle, low = parts3(work[:, width:])
        inverse = jnp.concatenate([high, high, high, middle, middle, low], axis=1)

        def solved(values):
            high, middle, low = parts3(values)
            stacked = jnp.concatenate([high, middle, low, high, middle, high], axis=0)
            return jnp.dot(inverse, stacked, preferred_element_type=jnp.float32)

        basis_ref[...] = solved(panel_ref[...]) * root_rows
        for j in range(0, count, LANES):
            size = min(LANES, count - j)
            start = j // LANES * width
            block = solved(summed_ref[start : start + width]) * (1.0 / root_rows)
            projection_ref[:, j : j + size] = block[:, :size]

    return pl.pallas_call(
        kernel,
        out_shape=(
            jax.ShapeDtypeStruct((width, cells), jnp.float32),
            jax.ShapeDtypeStruct((width, width), jnp.float32),
            jax.ShapeDtypeStruct((width, count), jnp.float32),
        ),
        compiler_params=pltpu.CompilerParams(vmem_limit_bytes=32 * MIB),
        name="results",
    )(summed, panel)


def spread(block, axes):
    copies = jnp.broadcast_to(block[None], (lax.axis_size(axes), *block.shape))
    return lax.all_to_all(copies, axes, 0, 0)


def body(snapshot_panel, following):
    root_rows = math.sqrt(snapshot_panel.shape[1] * lax.axis_size(AXES))
    products = local_products(snapshot_panel, following)
    chunks = products.reshape(lax.axis_size(PLANE), -1, LANES)
    mine = lax.all_to_all(chunks, PLANE, 0, 0).sum(axis=0)
    mine = spread(mine, "z").sum(axis=0)
    summed = spread(mine, PLANE).reshape(products.shape)
    return results(summed, snapshot_panel, root_rows)


def solution(mesh):
    mesh = Mesh(mesh.devices.reshape(SIZES), AXES)
    return jax.shard_map(
        body,
        mesh=mesh,
        in_specs=(P(None, AXES), P(None, AXES)),
        out_specs=(P(None, AXES), P(), P()),
        check_vma=False,
    )
```

```python
import math

import jax
import jax.numpy as jnp
import numpy as np
from jax import lax
from jax.experimental import pallas as pl
from jax.experimental.pallas import tpu as pltpu
from jax.sharding import Mesh
from jax.sharding import PartitionSpec as P

AXES = ("z", "y_lo", "y_hi", "x", "core")
SIZES = (8, 2, 2, 4, 2)
PLANE = AXES[1:]
LAST = (((1,), (1,)), ((), ()))
LANES = 128
MIB = 1 << 20
BLOCK = 8


def parts3(values):
    high = values.astype(jnp.bfloat16)
    rest = values - high.astype(jnp.float32)
    middle = rest.astype(jnp.bfloat16)
    return high, middle, (rest - middle.astype(jnp.float32)).astype(jnp.bfloat16)


def last_product(left, right):
    return lax.dot_general(left, right, LAST, preferred_element_type=jnp.float32)


def local_products(panel, following):
    width, cells = panel.shape
    count = following.shape[0]
    columns = count + width
    pieces = 4
    piece = cells // pieces

    def kernel(panel_hbm, following_hbm, out_ref, panel_v, following_v, stack, total, sem):
        def copy(i):
            cut = pl.ds(pl.multiple_of(i * piece, LANES), piece)
            return pltpu.make_async_copy(following_hbm.at[:, cut], following_v.at[i], sem.at[1 + i])

        panel_copy = pltpu.make_async_copy(panel_hbm, panel_v, sem.at[0])
        panel_copy.start()
        copy(0).start()
        panel_copy.wait()
        for i in range(1, pieces):
            copy(i).start()
        high, middle, low = parts3(panel_v[...])
        for i in range(pieces):
            cut = slice(i * piece, (i + 1) * piece)
            stack[i, :width] = high[:, cut]
            stack[i, width:] = middle[:, cut]
        whole = jnp.concatenate([high, middle, low], axis=0)
        sums = last_product(whole, high) + last_product(whole, middle) + last_product(whole, low)
        total[:, :count] = jnp.zeros((width, count), jnp.float32)
        total[:, count:] = sums[:width] + sums[width : 2 * width] + sums[2 * width :]

        @pl.loop(0, pieces)
        def _(i):
            copy(i).wait()
            values = following_v[i]
            high = values.astype(jnp.bfloat16)
            low = (values - high.astype(jnp.float32)).astype(jnp.bfloat16)
            sums = last_product(stack[i], high)
            total[:, :count] += sums[:width] + sums[width:] + last_product(stack[i, :width], low)

        for j in range(columns // LANES):
            out_ref[j * width : (j + 1) * width] = total[:, j * LANES : (j + 1) * LANES]

    return pl.pallas_call(
        kernel,
        out_shape=jax.ShapeDtypeStruct((width * columns // LANES, LANES), jnp.float32),
        in_specs=[pl.BlockSpec(memory_space=pltpu.HBM)] * 2,
        out_specs=pl.BlockSpec(memory_space=pltpu.VMEM),
        scratch_shapes=[
            pltpu.VMEM((width, cells), jnp.float32),
            pltpu.VMEM((pieces, count, piece), jnp.float32),
            pltpu.VMEM((pieces, 2 * width, piece), jnp.bfloat16),
            pltpu.VMEM((width, columns), jnp.float32),
            pltpu.SemaphoreType.DMA((1 + pieces,)),
        ],
        compiler_params=pltpu.CompilerParams(vmem_limit_bytes=54656 * 1024),
        name="local_products",
    )(panel, following)


def eliminated(work, width):
    done = []
    for base in range(0, width, BLOCK):
        left = width - base
        columns = [jnp.broadcast_to(work[:, base + j : base + j + 1], (left, 2 * width)) for j in range(BLOCK)]
        rows = [work[j : j + 1] for j in range(BLOCK)]
        corner = [[columns[j][i : i + 1] for j in range(BLOCK)] for i in range(BLOCK)]
        inverses = []
        for j in range(BLOCK):
            inverses.append(1.0 / corner[j][j])
            for i in range(j + 1, BLOCK):
                factor = corner[i][j] * inverses[j]
                rows[i] = rows[i] - factor * rows[j]
                for k in range(j + 1, BLOCK):
                    corner[i][k] = corner[i][k] - factor * corner[j][k]
        if left > BLOCK:
            below = [column[BLOCK:] for column in columns]
            work = work[BLOCK:]
            for j in range(BLOCK):
                work = work - below[j] * (rows[j] * inverses[j])
                for k in range(j + 1, BLOCK):
                    below[k] = below[k] - below[j] * (corner[j][k] * inverses[j])
        done += [rows[j] / jnp.sqrt(corner[j][j]) for j in range(BLOCK)]
    return jnp.concatenate(done, axis=0)


def stacked_left(high, middle, low):
    return jnp.concatenate([high, high, high, middle, middle, low], axis=1)


def stacked_right(values):
    high, middle, low = parts3(values)
    return jnp.concatenate([high, middle, low, high, middle, high], axis=0)


def factored(gram, panel, root_rows):
    width, cells = panel.shape

    def kernel(gram_ref, panel_ref, basis_ref, upper_ref, inverse_ref):
        rows = lax.broadcasted_iota(jnp.int32, (width, 2 * width), 0)
        lanes = lax.broadcasted_iota(jnp.int32, (width, 2 * width), 1)
        unit = jnp.where(lanes == rows + width, 1.0, 0.0)
        work = eliminated(jnp.where(lanes < width, pltpu.roll(gram_ref[...], width, axis=1), unit), width)
        upper_ref[...] = jnp.where(rows <= lanes, work, 0.0)[:, :width] * (1.0 / root_rows)
        inverse = stacked_left(*parts3(work[:, width:]))
        inverse_ref[...] = inverse
        basis = jnp.dot(inverse, stacked_right(panel_ref[...]), preferred_element_type=jnp.float32)
        basis_ref[...] = basis * root_rows

    return pl.pallas_call(
        kernel,
        out_shape=(
            jax.ShapeDtypeStruct((width, cells), jnp.float32),
            jax.ShapeDtypeStruct((width, width), jnp.float32),
            jax.ShapeDtypeStruct((width, 6 * width), jnp.bfloat16),
        ),
        compiler_params=pltpu.CompilerParams(vmem_limit_bytes=32 * MIB),
        name="factored",
    )(gram, panel)


def projected(inverse, summed, root_rows):
    width = inverse.shape[0]
    count = summed.shape[0] * LANES // width - width

    def kernel(inverse_ref, summed_ref, out_ref):
        for j in range(0, count, LANES):
            size = min(LANES, count - j)
            start = j // LANES * width
            right = stacked_right(summed_ref[start : start + width])
            block = jnp.dot(inverse_ref[...], right, preferred_element_type=jnp.float32) * (1.0 / root_rows)
            out_ref[:, j : j + size] = block[:, :size]

    return pl.pallas_call(
        kernel,
        out_shape=jax.ShapeDtypeStruct((width, count), jnp.float32),
        compiler_params=pltpu.CompilerParams(vmem_limit_bytes=32 * MIB),
        name="projected",
    )(inverse, summed)


def half_of(z, y, x, core):
    return core ^ ((x + y + z) % 2)


def exchange(block, *flips):
    pairs = []
    for index, (z, y_lo, y_hi, x, core) in enumerate(np.ndindex(*SIZES)):
        y = 2 * y_hi + y_lo
        half = half_of(z, y, x, core)
        fz, fy, fx = flips[half]
        tz, ty, tx = z ^ fz, y ^ fy, x ^ fx
        tc = half_of(tz, ty, tx, half)
        pairs.append((index, int(np.ravel_multi_index((tz, ty % 2, ty // 2, tx, tc), SIZES))))
    return lax.ppermute(block, AXES, pairs)


def other_core(block):
    return lax.ppermute(block, AXES, [(i, i ^ 1) for i in range(math.prod(SIZES))])


X1, X3, Y1, Y3, Z1, Z2, Z7 = (0, 0, 1), (0, 0, 3), (0, 1, 0), (0, 3, 0), (1, 0, 0), (2, 0, 0), (7, 0, 0)

ROUNDS = [((X1, Z7),) * 2, ((X3, Z1),) * 2, ((Y1, Z2),) * 2, ((Y3, X1),) * 2, ((Z7, X3),) * 2, ((Z1, Y1),) * 2, ((Z2, Y3),) * 2]


def body(snapshot_panel, following):
    root_rows = math.sqrt(snapshot_panel.shape[1] * lax.axis_size(AXES))
    products = local_products(snapshot_panel, following)
    halves = products.reshape(2, 2, -1, LANES)
    place = (lax.axis_index("z"), 2 * lax.axis_index("y_hi") + lax.axis_index("y_lo"), lax.axis_index("x"))
    half = half_of(*place, lax.axis_index("core"))
    mine = lax.dynamic_index_in_dim(halves, half, keepdims=False)
    theirs = lax.dynamic_index_in_dim(halves, 1 - half, keepdims=False)
    one = mine[1] + other_core(theirs[1])
    two = mine[0] + other_core(theirs[0])
    for first, second in ROUNDS:
        one = one + exchange(one, *first)
        two = two + exchange(two, *second)

    def both(block):
        other = other_core(block)
        return jnp.where(half == 0, block, other), jnp.where(half == 0, other, block)

    first, last = both(one)
    basis, upper, inverse = factored(last[-snapshot_panel.shape[0] :], snapshot_panel, root_rows)
    low, high = both(two)
    projection = projected(inverse, jnp.concatenate([low, first, high, last]), root_rows)
    return basis, upper, projection


def solution(mesh):
    mesh = Mesh(mesh.devices.reshape(SIZES), AXES)
    return jax.shard_map(
        body,
        mesh=mesh,
        in_specs=(P(None, AXES), P(None, AXES)),
        out_specs=(P(None, AXES), P(), P()),
        check_vma=False,
    )
```

```python
import math

import jax
import jax.numpy as jnp
import numpy as np
from jax import lax
from jax.experimental import pallas as pl
from jax.experimental.pallas import tpu as pltpu
from jax.sharding import Mesh
from jax.sharding import PartitionSpec as P

AXES = ("z", "y_lo", "y_hi", "x", "core")
SIZES = (8, 2, 2, 4, 2)
PLANE = AXES[1:]
LAST = (((1,), (1,)), ((), ()))
LANES = 128
MIB = 1 << 20
BLOCK = 8


def parts3(values):
    high = values.astype(jnp.bfloat16)
    rest = values - high.astype(jnp.float32)
    middle = rest.astype(jnp.bfloat16)
    return high, middle, (rest - middle.astype(jnp.float32)).astype(jnp.bfloat16)


def last_product(left, right):
    return lax.dot_general(left, right, LAST, preferred_element_type=jnp.float32)


def local_products(panel, following):
    width, cells = panel.shape
    count = following.shape[0]
    columns = count + width
    pieces = 4
    piece = cells // pieces

    def kernel(panel_hbm, following_hbm, out_ref, panel_v, following_v, stack, total, sem):
        def copy(i):
            cut = pl.ds(pl.multiple_of(i * piece, LANES), piece)
            return pltpu.make_async_copy(following_hbm.at[:, cut], following_v.at[i], sem.at[1 + i])

        panel_copy = pltpu.make_async_copy(panel_hbm, panel_v, sem.at[0])
        panel_copy.start()
        copy(0).start()
        panel_copy.wait()
        for i in range(1, pieces):
            copy(i).start()
        high, middle, low = parts3(panel_v[...])
        for i in range(pieces):
            cut = slice(i * piece, (i + 1) * piece)
            stack[i, :width] = high[:, cut]
            stack[i, width : 2 * width] = middle[:, cut]
            stack[i, 2 * width :] = low[:, cut]
        whole = jnp.concatenate([high, middle, low], axis=0)
        sums = last_product(whole, high) + last_product(whole, middle) + last_product(whole, low)
        total[:, :count] = jnp.zeros((width, count), jnp.float32)
        total[:, count:] = sums[:width] + sums[width : 2 * width] + sums[2 * width :]

        @pl.loop(0, pieces)
        def _(i):
            copy(i).wait()
            values = following_v[i]
            high = values.astype(jnp.bfloat16)
            low = (values - high.astype(jnp.float32)).astype(jnp.bfloat16)
            sums = last_product(stack[i], high) + last_product(stack[i], low)
            total[:, :count] += sums[:width] + sums[width : 2 * width] + sums[2 * width :]

        for j in range(columns // LANES):
            out_ref[j * width : (j + 1) * width] = total[:, j * LANES : (j + 1) * LANES]

    return pl.pallas_call(
        kernel,
        out_shape=jax.ShapeDtypeStruct((width * columns // LANES, LANES), jnp.float32),
        in_specs=[pl.BlockSpec(memory_space=pltpu.HBM)] * 2,
        out_specs=pl.BlockSpec(memory_space=pltpu.VMEM),
        scratch_shapes=[
            pltpu.VMEM((width, cells), jnp.float32),
            pltpu.VMEM((pieces, count, piece), jnp.float32),
            pltpu.VMEM((pieces, 3 * width, piece), jnp.bfloat16),
            pltpu.VMEM((width, columns), jnp.float32),
            pltpu.SemaphoreType.DMA((1 + pieces,)),
        ],
        compiler_params=pltpu.CompilerParams(vmem_limit_bytes=54656 * 1024),
        name="local_products",
    )(panel, following)


def eliminated(work, width):
    done = []
    for base in range(0, width, BLOCK):
        left = width - base
        columns = [jnp.broadcast_to(work[:, base + j : base + j + 1], (left, 2 * width)) for j in range(BLOCK)]
        rows = [work[j : j + 1] for j in range(BLOCK)]
        corner = [[columns[j][i : i + 1] for j in range(BLOCK)] for i in range(BLOCK)]
        inverses = []
        for j in range(BLOCK):
            inverses.append(1.0 / corner[j][j])
            for i in range(j + 1, BLOCK):
                factor = corner[i][j] * inverses[j]
                rows[i] = rows[i] - factor * rows[j]
                for k in range(j + 1, BLOCK):
                    corner[i][k] = corner[i][k] - factor * corner[j][k]
        if left > BLOCK:
            below = [column[BLOCK:] for column in columns]
            work = work[BLOCK:]
            for j in range(BLOCK):
                work = work - below[j] * (rows[j] * inverses[j])
                for k in range(j + 1, BLOCK):
                    below[k] = below[k] - below[j] * (corner[j][k] * inverses[j])
        done += [rows[j] / jnp.sqrt(corner[j][j]) for j in range(BLOCK)]
    return jnp.concatenate(done, axis=0)


def stacked_left(high, middle, low):
    return jnp.concatenate([high, high, high, middle, middle, low], axis=1)


def stacked_right(values):
    high, middle, low = parts3(values)
    return jnp.concatenate([high, middle, low, high, middle, high], axis=0)


def factored(gram, panel, root_rows):
    width, cells = panel.shape

    def kernel(gram_ref, panel_ref, basis_ref, upper_ref, inverse_ref):
        rows = lax.broadcasted_iota(jnp.int32, (width, 2 * width), 0)
        lanes = lax.broadcasted_iota(jnp.int32, (width, 2 * width), 1)
        unit = jnp.where(lanes == rows + width, 1.0, 0.0)
        work = eliminated(jnp.where(lanes < width, pltpu.roll(gram_ref[...], width, axis=1), unit), width)
        upper_ref[...] = jnp.where(rows <= lanes, work, 0.0)[:, :width] * (1.0 / root_rows)
        inverse = stacked_left(*parts3(work[:, width:]))
        inverse_ref[...] = inverse
        basis = jnp.dot(inverse, stacked_right(panel_ref[...]), preferred_element_type=jnp.float32)
        basis_ref[...] = basis * root_rows

    return pl.pallas_call(
        kernel,
        out_shape=(
            jax.ShapeDtypeStruct((width, cells), jnp.float32),
            jax.ShapeDtypeStruct((width, width), jnp.float32),
            jax.ShapeDtypeStruct((width, 6 * width), jnp.bfloat16),
        ),
        compiler_params=pltpu.CompilerParams(vmem_limit_bytes=32 * MIB),
        name="factored",
    )(gram, panel)


def projected(inverse, summed, root_rows):
    width = inverse.shape[0]
    count = summed.shape[0] * LANES // width - width

    def kernel(inverse_ref, summed_ref, out_ref):
        for j in range(0, count, LANES):
            size = min(LANES, count - j)
            start = j // LANES * width
            right = stacked_right(summed_ref[start : start + width])
            block = jnp.dot(inverse_ref[...], right, preferred_element_type=jnp.float32) * (1.0 / root_rows)
            out_ref[:, j : j + size] = block[:, :size]

    return pl.pallas_call(
        kernel,
        out_shape=jax.ShapeDtypeStruct((width, count), jnp.float32),
        compiler_params=pltpu.CompilerParams(vmem_limit_bytes=32 * MIB),
        name="projected",
    )(inverse, summed)


def half_of(z, y, x, core):
    return core ^ ((x + y + z) % 2)


def exchange(block, *flips):
    pairs = []
    for index, (z, y_lo, y_hi, x, core) in enumerate(np.ndindex(*SIZES)):
        y = 2 * y_hi + y_lo
        half = half_of(z, y, x, core)
        fz, fy, fx = flips[half]
        tz, ty, tx = z ^ fz, y ^ fy, x ^ fx
        tc = half_of(tz, ty, tx, half)
        pairs.append((index, int(np.ravel_multi_index((tz, ty % 2, ty // 2, tx, tc), SIZES))))
    return lax.ppermute(block, AXES, pairs)


def other_core(block):
    return lax.ppermute(block, AXES, [(i, i ^ 1) for i in range(math.prod(SIZES))])


X1, X3, Y1, Y3, Z1, Z2, Z7 = (0, 0, 1), (0, 0, 3), (0, 1, 0), (0, 3, 0), (1, 0, 0), (2, 0, 0), (7, 0, 0)

ROUNDS = [((X1, Z1),) * 2, ((Z1, X1),) * 2, ((Y1, Z2),) * 2, ((X3, Y1),) * 2, ((Y3, Z7),) * 2, ((Z2, X3),) * 2, ((Z7, Y3),) * 2]


def body(snapshot_panel, following):
    root_rows = math.sqrt(snapshot_panel.shape[1] * lax.axis_size(AXES))
    products = local_products(snapshot_panel, following)
    halves = products.reshape(2, 2, -1, LANES)
    place = (lax.axis_index("z"), 2 * lax.axis_index("y_hi") + lax.axis_index("y_lo"), lax.axis_index("x"))
    half = half_of(*place, lax.axis_index("core"))
    mine = lax.dynamic_index_in_dim(halves, half, keepdims=False)
    theirs = lax.dynamic_index_in_dim(halves, 1 - half, keepdims=False)
    one = mine[1] + other_core(theirs[1])
    two = mine[0] + other_core(theirs[0])
    for first, second in ROUNDS:
        one = one + exchange(one, *first)
        two = two + exchange(two, *second)

    def both(block):
        other = other_core(block)
        return jnp.where(half == 0, block, other), jnp.where(half == 0, other, block)

    first, last = both(one)
    basis, upper, inverse = factored(last[-snapshot_panel.shape[0] :], snapshot_panel, root_rows)
    low, high = both(two)
    projection = projected(inverse, jnp.concatenate([low, first, high, last]), root_rows)
    return basis, upper, projection


def solution(mesh):
    mesh = Mesh(mesh.devices.reshape(SIZES), AXES)
    return jax.shard_map(
        body,
        mesh=mesh,
        in_specs=(P(None, AXES), P(None, AXES)),
        out_specs=(P(None, AXES), P(), P()),
        check_vma=False,
    )
```

```python
import math

import jax
import jax.numpy as jnp
import numpy as np
from jax import lax
from jax.experimental import pallas as pl
from jax.experimental.pallas import tpu as pltpu
from jax.sharding import Mesh
from jax.sharding import PartitionSpec as P

AXES = ("z", "y_lo", "y_hi", "x", "core")
SIZES = (8, 2, 2, 4, 2)
PLANE = AXES[1:]
LAST = (((1,), (1,)), ((), ()))
LANES = 128
MIB = 1 << 20
BLOCK = 8


def parts3(values):
    high = values.astype(jnp.bfloat16)
    rest = values - high.astype(jnp.float32)
    middle = rest.astype(jnp.bfloat16)
    return high, middle, (rest - middle.astype(jnp.float32)).astype(jnp.bfloat16)


def last_product(left, right):
    return lax.dot_general(left, right, LAST, preferred_element_type=jnp.float32)


def local_products(panel, following):
    width, cells = panel.shape
    count = following.shape[0]
    columns = count + width
    pieces = 4
    piece = cells // pieces

    def kernel(panel_hbm, following_hbm, out_ref, panel_v, following_v, stack, total, sem):
        def copy(i):
            cut = pl.ds(pl.multiple_of(i * piece, LANES), piece)
            return pltpu.make_async_copy(following_hbm.at[:, cut], following_v.at[i], sem.at[1 + i])

        panel_copy = pltpu.make_async_copy(panel_hbm, panel_v, sem.at[0])
        panel_copy.start()
        copy(0).start()
        panel_copy.wait()
        for i in range(1, pieces):
            copy(i).start()
        high, middle, low = parts3(panel_v[...])
        for i in range(pieces):
            cut = slice(i * piece, (i + 1) * piece)
            stack[i, :width] = high[:, cut]
            stack[i, width : 2 * width] = middle[:, cut]
            stack[i, 2 * width :] = low[:, cut]
        whole = jnp.concatenate([high, middle, low], axis=0)
        sums = last_product(whole, high) + last_product(whole, middle) + last_product(whole, low)
        total[:, :count] = jnp.zeros((width, count), jnp.float32)
        total[:, count:] = sums[:width] + sums[width : 2 * width] + sums[2 * width :]

        @pl.loop(0, pieces)
        def _(i):
            copy(i).wait()
            values = following_v[i]
            high = values.astype(jnp.bfloat16)
            low = (values - high.astype(jnp.float32)).astype(jnp.bfloat16)
            sums = last_product(stack[i], high) + last_product(stack[i], low)
            total[:, :count] += sums[:width] + sums[width : 2 * width] + sums[2 * width :]

        for j in range(columns // LANES):
            out_ref[j * width : (j + 1) * width] = total[:, j * LANES : (j + 1) * LANES]

    return pl.pallas_call(
        kernel,
        out_shape=jax.ShapeDtypeStruct((width * columns // LANES, LANES), jnp.float32),
        in_specs=[pl.BlockSpec(memory_space=pltpu.HBM)] * 2,
        out_specs=pl.BlockSpec(memory_space=pltpu.VMEM),
        scratch_shapes=[
            pltpu.VMEM((width, cells), jnp.float32),
            pltpu.VMEM((pieces, count, piece), jnp.float32),
            pltpu.VMEM((pieces, 3 * width, piece), jnp.bfloat16),
            pltpu.VMEM((width, columns), jnp.float32),
            pltpu.SemaphoreType.DMA((1 + pieces,)),
        ],
        compiler_params=pltpu.CompilerParams(vmem_limit_bytes=54656 * 1024),
        name="local_products",
    )(panel, following)


def eliminated(work, width):
    done = []
    for base in range(0, width, BLOCK):
        left = width - base
        columns = [jnp.broadcast_to(work[:, base + j : base + j + 1], (left, 2 * width)) for j in range(BLOCK)]
        rows = [work[j : j + 1] for j in range(BLOCK)]
        corner = [[columns[j][i : i + 1] for j in range(BLOCK)] for i in range(BLOCK)]
        inverses = []
        for j in range(BLOCK):
            inverses.append(1.0 / corner[j][j])
            for i in range(j + 1, BLOCK):
                factor = corner[i][j] * inverses[j]
                rows[i] = rows[i] - factor * rows[j]
                for k in range(j + 1, BLOCK):
                    corner[i][k] = corner[i][k] - factor * corner[j][k]
        if left > BLOCK:
            below = [column[BLOCK:] for column in columns]
            work = work[BLOCK:]
            for j in range(BLOCK):
                work = work - below[j] * (rows[j] * inverses[j])
                for k in range(j + 1, BLOCK):
                    below[k] = below[k] - below[j] * (corner[j][k] * inverses[j])
        done += [rows[j] / jnp.sqrt(corner[j][j]) for j in range(BLOCK)]
    return jnp.concatenate(done, axis=0)


def stacked_left(high, middle, low):
    return jnp.concatenate([high, high, high, middle, middle, low], axis=1)


def stacked_right(values):
    high, middle, low = parts3(values)
    return jnp.concatenate([high, middle, low, high, middle, high], axis=0)


def factored(half, own, other, width, root_rows):
    start = own.shape[0] - width

    def kernel(half_ref, own_ref, other_ref, upper_ref, inverse_ref):
        rows = lax.broadcasted_iota(jnp.int32, (width, 2 * width), 0)
        lanes = lax.broadcasted_iota(jnp.int32, (width, 2 * width), 1)
        unit = jnp.where(lanes == rows + width, 1.0, 0.0)
        block = jnp.where(half_ref[0] == 1, own_ref[start:], other_ref[start:])
        work = eliminated(jnp.where(lanes < width, pltpu.roll(block, width, axis=1), unit), width)
        upper_ref[...] = jnp.where(rows <= lanes, work, 0.0)[:, :width] * (1.0 / root_rows)
        inverse_ref[...] = stacked_left(*parts3(work[:, width:]))

    return pl.pallas_call(
        kernel,
        out_shape=(
            jax.ShapeDtypeStruct((width, width), jnp.float32),
            jax.ShapeDtypeStruct((width, 6 * width), jnp.bfloat16),
        ),
        in_specs=[pl.BlockSpec(memory_space=pltpu.SMEM)] + [pl.BlockSpec(memory_space=pltpu.VMEM)] * 2,
        compiler_params=pltpu.CompilerParams(vmem_limit_bytes=32 * MIB),
        name="factored",
    )(half, own, other)


def solved(half, inverse, panel, sums, root_rows):
    width = inverse.shape[0]
    quarter = sums[0][0].shape[0]
    count = 4 * quarter * LANES // width - width

    def kernel(half_ref, inverse_ref, panel_ref, own0, other0, own1, other1, basis_hbm, out_hbm, basis, out, sem):
        basis[...] = (
            jnp.dot(inverse_ref[...], stacked_right(panel_ref[...]), preferred_element_type=jnp.float32) * root_rows
        )
        basis_copy = pltpu.make_async_copy(basis, basis_hbm, sem.at[0])
        basis_copy.start()
        for j in range(0, count, LANES):
            size = min(LANES, count - j)
            place, start = divmod(j // LANES * width, quarter)
            own, other = ((own0, other0), (own1, other1))[place % 2]
            rows = slice(start, start + width)
            right = stacked_right(jnp.where(half_ref[0] == place // 2, own[rows], other[rows]))
            block = jnp.dot(inverse_ref[...], right, preferred_element_type=jnp.float32) * (1.0 / root_rows)
            out[:, j : j + size] = block[:, :size]
        out_copy = pltpu.make_async_copy(out, out_hbm, sem.at[1])
        out_copy.start()
        basis_copy.wait()
        out_copy.wait()

    return pl.pallas_call(
        kernel,
        out_shape=(
            jax.ShapeDtypeStruct(panel.shape, jnp.float32),
            jax.ShapeDtypeStruct((width, count), jnp.float32),
        ),
        in_specs=[pl.BlockSpec(memory_space=pltpu.SMEM)] + [pl.BlockSpec(memory_space=pltpu.VMEM)] * 6,
        out_specs=(pl.BlockSpec(memory_space=pltpu.HBM),) * 2,
        scratch_shapes=[
            pltpu.VMEM(panel.shape, jnp.float32),
            pltpu.VMEM((width, count), jnp.float32),
            pltpu.SemaphoreType.DMA((2,)),
        ],
        compiler_params=pltpu.CompilerParams(vmem_limit_bytes=32 * MIB),
        name="solved",
    )(half, inverse, panel, *sums[0], *sums[1])


def half_of(z, y, x, core):
    return core ^ ((x + y + z) % 2)


def exchange(block, *flips):
    pairs = []
    for index, (z, y_lo, y_hi, x, core) in enumerate(np.ndindex(*SIZES)):
        y = 2 * y_hi + y_lo
        half = half_of(z, y, x, core)
        fz, fy, fx = flips[half]
        tz, ty, tx = z ^ fz, y ^ fy, x ^ fx
        tc = half_of(tz, ty, tx, half)
        pairs.append((index, int(np.ravel_multi_index((tz, ty % 2, ty // 2, tx, tc), SIZES))))
    return lax.ppermute(block, AXES, pairs)


def other_core(block):
    return lax.ppermute(block, AXES, [(i, i ^ 1) for i in range(math.prod(SIZES))])


X1, X3, Y1, Y3, Z1, Z2, Z7 = (0, 0, 1), (0, 0, 3), (0, 1, 0), (0, 3, 0), (1, 0, 0), (2, 0, 0), (7, 0, 0)

ROUNDS = [((X1, Z1),) * 2, ((Z1, X1),) * 2, ((Y1, Z2),) * 2, ((X3, Y1),) * 2, ((Y3, Z7),) * 2, ((Z2, X3),) * 2, ((Z7, Y3),) * 2]


def body(snapshot_panel, following):
    root_rows = math.sqrt(snapshot_panel.shape[1] * lax.axis_size(AXES))
    products = local_products(snapshot_panel, following)
    halves = products.reshape(2, 2, -1, LANES)
    place = (lax.axis_index("z"), 2 * lax.axis_index("y_hi") + lax.axis_index("y_lo"), lax.axis_index("x"))
    half = half_of(*place, lax.axis_index("core"))
    mine = lax.dynamic_index_in_dim(halves, half, keepdims=False)
    theirs = lax.dynamic_index_in_dim(halves, 1 - half, keepdims=False)
    one = mine[1] + other_core(theirs[1])
    two = mine[0] + other_core(theirs[0])
    for first, second in ROUNDS:
        one = one + exchange(one, *first)
        two = two + exchange(two, *second)

    flag = half.astype(jnp.int32).reshape(1)
    one = one, other_core(one)
    upper, inverse = factored(flag, *one, snapshot_panel.shape[0], root_rows)
    two = two, other_core(two)
    basis, projection = solved(flag, inverse, snapshot_panel, (two, one), root_rows)
    return basis, upper, projection


def solution(mesh):
    mesh = Mesh(mesh.devices.reshape(SIZES), AXES)
    return jax.shard_map(
        body,
        mesh=mesh,
        in_specs=(P(None, AXES), P(None, AXES)),
        out_specs=(P(None, AXES), P(), P()),
        check_vma=False,
    )
```

```python
import math

import jax
import jax.numpy as jnp
import numpy as np
from jax import lax
from jax.experimental import pallas as pl
from jax.experimental.pallas import tpu as pltpu
from jax.sharding import Mesh
from jax.sharding import PartitionSpec as P

AXES = ("z", "y_lo", "y_hi", "x", "core")
SIZES = (8, 2, 2, 4, 2)
PLANE = AXES[1:]
LAST = (((1,), (1,)), ((), ()))
LANES = 128
MIB = 1 << 20
BLOCK = 8


def parts3(values):
    high = values.astype(jnp.bfloat16)
    rest = values - high.astype(jnp.float32)
    middle = rest.astype(jnp.bfloat16)
    return high, middle, (rest - middle.astype(jnp.float32)).astype(jnp.bfloat16)


def last_product(left, right):
    return lax.dot_general(left, right, LAST, preferred_element_type=jnp.float32)


def local_products(panel, following):
    width, cells = panel.shape
    count = following.shape[0]
    columns = count + width
    pieces = 4
    piece = cells // pieces

    def kernel(panel_hbm, following_hbm, out_ref, panel_v, following_v, stack, total, sem):
        def copy(i):
            cut = pl.ds(pl.multiple_of(i * piece, LANES), piece)
            return pltpu.make_async_copy(following_hbm.at[:, cut], following_v.at[i], sem.at[1 + i])

        panel_copy = pltpu.make_async_copy(panel_hbm, panel_v, sem.at[0])
        panel_copy.start()
        copy(0).start()
        panel_copy.wait()
        for i in range(1, pieces):
            copy(i).start()
        high, middle, low = parts3(panel_v[...])
        for i in range(pieces):
            cut = slice(i * piece, (i + 1) * piece)
            stack[i, :width] = high[:, cut]
            stack[i, width : 2 * width] = middle[:, cut]
            stack[i, 2 * width :] = low[:, cut]
        whole = jnp.concatenate([high, middle, low], axis=0)
        sums = last_product(whole, high) + last_product(whole, middle) + last_product(whole, low)
        total[:, :count] = jnp.zeros((width, count), jnp.float32)
        total[:, count:] = sums[:width] + sums[width : 2 * width] + sums[2 * width :]

        @pl.loop(0, pieces)
        def _(i):
            copy(i).wait()
            values = following_v[i]
            high = values.astype(jnp.bfloat16)
            low = (values - high.astype(jnp.float32)).astype(jnp.bfloat16)
            sums = last_product(stack[i], high) + last_product(stack[i], low)
            total[:, :count] += sums[:width] + sums[width : 2 * width] + sums[2 * width :]

        for j in range(columns // LANES):
            out_ref[j * width : (j + 1) * width] = total[:, j * LANES : (j + 1) * LANES]

    return pl.pallas_call(
        kernel,
        out_shape=jax.ShapeDtypeStruct((width * columns // LANES, LANES), jnp.float32),
        in_specs=[pl.BlockSpec(memory_space=pltpu.HBM)] * 2,
        out_specs=pl.BlockSpec(memory_space=pltpu.VMEM),
        scratch_shapes=[
            pltpu.VMEM((width, cells), jnp.float32),
            pltpu.VMEM((pieces, count, piece), jnp.float32),
            pltpu.VMEM((pieces, 3 * width, piece), jnp.bfloat16),
            pltpu.VMEM((width, columns), jnp.float32),
            pltpu.SemaphoreType.DMA((1 + pieces,)),
        ],
        compiler_params=pltpu.CompilerParams(vmem_limit_bytes=54656 * 1024),
        name="local_products",
    )(panel, following)


def eliminated(work, width):
    done = []
    for base in range(0, width, BLOCK):
        left = width - base
        columns = [jnp.broadcast_to(work[:, base + j : base + j + 1], (left, 2 * width)) for j in range(BLOCK)]
        rows = [work[j : j + 1] for j in range(BLOCK)]
        corner = [[columns[j][i : i + 1] for j in range(BLOCK)] for i in range(BLOCK)]
        inverses = []
        for j in range(BLOCK):
            inverses.append(pl.reciprocal(corner[j][j]))
            for i in range(j + 1, BLOCK):
                factor = corner[i][j] * inverses[j]
                rows[i] = rows[i] - factor * rows[j]
                for k in range(j + 1, BLOCK):
                    corner[i][k] = corner[i][k] - factor * corner[j][k]
        if left > BLOCK:
            below = [column[BLOCK:] for column in columns]
            work = work[BLOCK:]
            for j in range(BLOCK):
                work = work - below[j] * (rows[j] * inverses[j])
                for k in range(j + 1, BLOCK):
                    below[k] = below[k] - below[j] * (corner[j][k] * inverses[j])
        done += [rows[j] / jnp.sqrt(corner[j][j]) for j in range(BLOCK)]
    return jnp.concatenate(done, axis=0)


def stacked_left(high, middle, low):
    return jnp.concatenate([high, high, high, middle, middle, low], axis=1)


def stacked_right(values):
    high, middle, low = parts3(values)
    return jnp.concatenate([high, middle, low, high, middle, high], axis=0)


def factored(half, own, other, width, root_rows):
    start = own.shape[0] - width

    def kernel(half_ref, own_ref, other_ref, upper_ref, inverse_ref):
        rows = lax.broadcasted_iota(jnp.int32, (width, 2 * width), 0)
        lanes = lax.broadcasted_iota(jnp.int32, (width, 2 * width), 1)
        unit = jnp.where(lanes == rows + width, 1.0, 0.0)
        block = jnp.where(half_ref[0] == 1, own_ref[start:], other_ref[start:])
        work = eliminated(jnp.where(lanes < width, pltpu.roll(block, width, axis=1), unit), width)
        upper_ref[...] = jnp.where(rows <= lanes, work, 0.0)[:, :width] * (1.0 / root_rows)
        inverse_ref[...] = stacked_left(*parts3(work[:, width:]))

    return pl.pallas_call(
        kernel,
        out_shape=(
            jax.ShapeDtypeStruct((width, width), jnp.float32),
            jax.ShapeDtypeStruct((width, 6 * width), jnp.bfloat16),
        ),
        in_specs=[pl.BlockSpec(memory_space=pltpu.SMEM)] + [pl.BlockSpec(memory_space=pltpu.VMEM)] * 2,
        compiler_params=pltpu.CompilerParams(vmem_limit_bytes=32 * MIB),
        name="factored",
    )(half, own, other)


def solved(half, inverse, panel, sums, root_rows):
    width = inverse.shape[0]
    quarter = sums[0][0].shape[0]
    count = 4 * quarter * LANES // width - width

    def kernel(half_ref, inverse_ref, panel_ref, own0, other0, own1, other1, basis_hbm, out_hbm, basis, out, sem):
        basis[...] = (
            jnp.dot(inverse_ref[...], stacked_right(panel_ref[...]), preferred_element_type=jnp.float32) * root_rows
        )
        basis_copy = pltpu.make_async_copy(basis, basis_hbm, sem.at[0])
        basis_copy.start()
        for j in range(0, count, LANES):
            size = min(LANES, count - j)
            place, start = divmod(j // LANES * width, quarter)
            own, other = ((own0, other0), (own1, other1))[place % 2]
            rows = slice(start, start + width)
            right = stacked_right(jnp.where(half_ref[0] == place // 2, own[rows], other[rows]))
            block = jnp.dot(inverse_ref[...], right, preferred_element_type=jnp.float32) * (1.0 / root_rows)
            out[:, j : j + size] = block[:, :size]
        out_copy = pltpu.make_async_copy(out, out_hbm, sem.at[1])
        out_copy.start()
        basis_copy.wait()
        out_copy.wait()

    return pl.pallas_call(
        kernel,
        out_shape=(
            jax.ShapeDtypeStruct(panel.shape, jnp.float32),
            jax.ShapeDtypeStruct((width, count), jnp.float32),
        ),
        in_specs=[pl.BlockSpec(memory_space=pltpu.SMEM)] + [pl.BlockSpec(memory_space=pltpu.VMEM)] * 6,
        out_specs=(pl.BlockSpec(memory_space=pltpu.HBM),) * 2,
        scratch_shapes=[
            pltpu.VMEM(panel.shape, jnp.float32),
            pltpu.VMEM((width, count), jnp.float32),
            pltpu.SemaphoreType.DMA((2,)),
        ],
        compiler_params=pltpu.CompilerParams(vmem_limit_bytes=32 * MIB),
        name="solved",
    )(half, inverse, panel, *sums[0], *sums[1])


def half_of(z, y, x, core):
    return core ^ ((x + y + z) % 2)


def exchange(block, *flips):
    pairs = []
    for index, (z, y_lo, y_hi, x, core) in enumerate(np.ndindex(*SIZES)):
        y = 2 * y_hi + y_lo
        half = half_of(z, y, x, core)
        fz, fy, fx = flips[half]
        tz, ty, tx = z ^ fz, y ^ fy, x ^ fx
        tc = half_of(tz, ty, tx, half)
        pairs.append((index, int(np.ravel_multi_index((tz, ty % 2, ty // 2, tx, tc), SIZES))))
    return lax.ppermute(block, AXES, pairs)


def other_core(block):
    return lax.ppermute(block, AXES, [(i, i ^ 1) for i in range(math.prod(SIZES))])


X1, X3, Y1, Y3, Z1, Z2, Z7 = (0, 0, 1), (0, 0, 3), (0, 1, 0), (0, 3, 0), (1, 0, 0), (2, 0, 0), (7, 0, 0)

ROUNDS = [((X1, Z1),) * 2, ((Z1, X1),) * 2, ((Y1, Z2),) * 2, ((X3, Y1),) * 2, ((Y3, Z7),) * 2, ((Z2, X3),) * 2, ((Z7, Y3),) * 2]


def body(snapshot_panel, following):
    root_rows = math.sqrt(snapshot_panel.shape[1] * lax.axis_size(AXES))
    products = local_products(snapshot_panel, following)
    halves = products.reshape(2, 2, -1, LANES)
    place = (lax.axis_index("z"), 2 * lax.axis_index("y_hi") + lax.axis_index("y_lo"), lax.axis_index("x"))
    half = half_of(*place, lax.axis_index("core"))
    mine = lax.dynamic_index_in_dim(halves, half, keepdims=False)
    theirs = lax.dynamic_index_in_dim(halves, 1 - half, keepdims=False)
    one = mine[1] + other_core(theirs[1])
    sent, _ = lax.optimization_barrier((theirs[0], one))
    two = mine[0] + other_core(sent)
    for first, second in ROUNDS:
        one = one + exchange(one, *first)
        two = two + exchange(two, *second)

    flag = half.astype(jnp.int32).reshape(1)
    one = one, other_core(one)
    upper, inverse = factored(flag, *one, snapshot_panel.shape[0], root_rows)
    two = two, other_core(two)
    basis, projection = solved(flag, inverse, snapshot_panel, (two, one), root_rows)
    return basis, upper, projection


def solution(mesh):
    mesh = Mesh(mesh.devices.reshape(SIZES), AXES)
    return jax.shard_map(
        body,
        mesh=mesh,
        in_specs=(P(None, AXES), P(None, AXES)),
        out_specs=(P(None, AXES), P(), P()),
        check_vma=False,
    )
```
